32 devices in a mesh: tiles: 8 (over z, x), rep: 4 (over y, core).
Axes of the slice: x: 2, y: 2, z: 4, core: 2. Of those that a mesh axis runs over, the one named last changes fastest.
Arguments:
- affinity: bfloat16 [128, 512, 512], P(('tiles', 'rep')), may hold values from -0.25 to 0.25
- tile_pairs: int32 [128, 2], P(('tiles', 'rep')), may hold values from 0 to 31, as said below
- factors: float32 [32, 512, 256], P('tiles'), may hold values from -6 to 6
Outputs:
- polar_factors: float32 [32, 512, 256], P('tiles')
The draws below stay inside these ranges and needn't reach their ends.
Inputs may be any that keep to these rules, and one draw needn't show every extreme that they name: `tile_pairs`: column 0 of a row is an image owned by the index of tiles that holds the row (images o * 4 to (o + 1) * 4 - 1 belong to index o); column 1 differs from column 0 by 1 to 4, and by exactly 4 in the first row held by every index of tiles.
All inputs are finite; a program needn't handle non-finite values.
Results may differ from the reference program's by a relative error of at most 0.0022.
Values may be sent and summed in bfloat16 or wider, within the bound.
A program may use at most 64 MiB of HBM per device.

```python
import math
import jax
import jax.numpy as jnp
from jax import lax

P_SIZE = 512
U = 256
IMG_DEV = 4
ROUNDS = 1
NS_STEPS = 6
IMAGES = 32
TILES = 128


def draw_tile_pairs(key, part):
    per_owner = TILES // (IMAGES // IMG_DEV)
    row_ids = jnp.arange(TILES, dtype=jnp.int32)
    owner = row_ids // per_owner
    keys = jax.random.split(jax.random.fold_in(key, 11), 4)
    first_pick = jnp.minimum(jax.random.randint(keys[0], (TILES,), 0, IMG_DEV), jax.random.randint(keys[1], (TILES,), 0, IMG_DEV))
    first_image = owner * IMG_DEV + first_pick
    offset = jax.random.randint(keys[2], (TILES,), 1, IMG_DEV + 1)
    offset = jnp.where(row_ids % per_owner == 0, IMG_DEV, offset)
    direction = jax.random.randint(keys[3], (TILES,), 0, 2) * 2 - 1
    second_image = first_image + direction * offset
    outside = (second_image < 0) | (second_image >= IMAGES)
    second_image = jnp.where(outside, first_image - direction * offset, second_image)
    return jnp.stack([first_image, second_image], axis=1).astype(jnp.int32)


def draw_factors(key, part):
    keys = jax.random.split(jax.random.fold_in(key, 23), 1)
    values = jax.random.normal(keys[0], (IMAGES, P_SIZE, U), jnp.float32)
    return jnp.clip(values, -6.0, 6.0)


def levels(rng, dims, cuts, low, largest):
    gain = 1.0
    for position, blocks in cuts:
        steps = jax.random.uniform(jax.random.fold_in(jax.random.fold_in(rng, 6), position), (blocks,), jnp.float32, low / len(cuts), largest / len(cuts))
        gain = gain * jnp.repeat(jnp.exp(steps), dims[position] // blocks).reshape((-1,) + (1,) * (len(dims) - 1 - position))
    return gain


def normal_values(own_key, shape, deviation, limit, cuts=(), held_as=jnp.bfloat16):
    result = deviation * jax.random.normal(own_key, shape, jnp.float32)
    if cuts:
        result = result * levels(own_key, shape, cuts, -0.22, 0.18)
    return jnp.clip(result, -limit, limit).astype(held_as)


def setup_inputs(seed: int = 0) -> dict:
    seeds = jax.random.split(jax.random.key(seed), 4)
    affinity = normal_values(seeds[0], (TILES, P_SIZE, P_SIZE), P_SIZE ** -0.5, 0.25, ((0, 32),))
    tile_pairs = draw_tile_pairs(jax.random.fold_in(seeds[3], 71), 0)
    factors = draw_factors(jax.random.fold_in(seeds[3], 71), 0)
    return dict(affinity=affinity, tile_pairs=tile_pairs, factors=factors)


epsilon = 1e-06
start_scale = 0.25
ascent_step = 0.25

def polar_project(ascended):
    iterate = ascended
    for sweep_index in range(NS_STEPS):
        gram_matrix = jnp.einsum('npu,npv->nuv', iterate, iterate, precision=lax.Precision.HIGHEST)
        if sweep_index == 0:
            squares = jnp.trace(gram_matrix, axis1=1, axis2=2)[:, None, None]
            factor = start_scale * math.sqrt(iterate.shape[2]) * lax.rsqrt(squares + epsilon)
            iterate = iterate * factor
            gram_matrix = gram_matrix * (factor * factor)
        iterate = 1.5 * iterate - 0.5 * jnp.einsum('npu,nuv->npv', iterate, gram_matrix, precision=lax.Precision.HIGHEST)
    return iterate * math.sqrt(P_SIZE)

def reference(affinity, tile_pairs, factors):
    current = factors
    for round_index in range(ROUNDS):
        rounded = current.astype(jnp.bfloat16)

        def accumulate(total, item):
            tile, pair = item
            first_image = lax.dynamic_index_in_dim(rounded, pair[0], 0, keepdims=False)
            second_image = lax.dynamic_index_in_dim(rounded, pair[1], 0, keepdims=False)
            forward = jnp.dot(tile, second_image, preferred_element_type=jnp.float32)
            backward = jnp.dot(tile.T, first_image, preferred_element_type=jnp.float32)
            total = total.at[pair[0]].add(forward)
            total = total.at[pair[1]].add(backward)
            return (total, None)
        gradient, unused = lax.scan(accumulate, jnp.zeros(current.shape, jnp.float32), (affinity, tile_pairs))
        current = polar_project(current + ascent_step * gradient)
    return current
```

```python
import functools
import math

import jax
import jax.numpy as jnp
from jax import lax
from jax.experimental import pallas as pl
from jax.experimental.pallas import tpu as pltpu
from jax.sharding import PartitionSpec as P

NS_STEPS = 6

epsilon = 1e-06
start_scale = 0.25
ascent_step = 0.25

CHUNKS = 2
LEFT, RIGHT, OWN = 0, 1, 2


def dot(a, b):
    return jnp.dot(a, b, preferred_element_type=jnp.float32)


def dot_t(a, b):
    return lax.dot_general(a, b, (((0,), (0,)), ((), ())), preferred_element_type=jnp.float32)


def split(x):
    high = x.astype(jnp.bfloat16)
    return high, (x - high.astype(jnp.float32)).astype(jnp.bfloat16)


def dot3(a, b):
    return dot(a[0], b[0]) + (dot(a[0], b[1]) + dot(a[1], b[0]))


def kernel(
    owners, rep, pairs_ref, aff_hbm, fac_hbm, out_ref, own_ref,
    aff, fac, held, win, back, forw, s1, r1, s2, r2, s3, r3, asc,
    load_sem, wx_s, wx_r, wy_s, wy_r, wc_s, wc_r,
    g1_s, g1_r, g2_s, g2_r, g3_s, g3_r, oy_s, oy_r, oc_s, oc_r,
):
    count, keypoints, universe = fac.shape
    tiles = aff.shape[0]
    pairs = rep // 2
    t = lax.axis_index("tiles")
    r = lax.axis_index("rep")
    p, c = r // 2, r % 2
    sibling = {"rep": 2 * p + (1 - c)}
    has = (t > 0, t < owners - 1)
    towards = ({"tiles": t - 1}, {"tiles": t + 1})
    rows_of = [
        pl.ds(i * (keypoints // CHUNKS), keypoints // CHUNKS) for i in range(CHUNKS)
    ]
    sent = []

    def pair_at(d):
        return lax.rem(p + d, pairs)

    def across(d):
        return {"rep": 2 * pair_at(d) + c}

    def send(src, dst, ssem, rsem, device, when=None):
        copy = pltpu.make_async_remote_copy(
            src_ref=src, dst_ref=dst, send_sem=ssem, recv_sem=rsem,
            device_id=device, device_id_type=pl.DeviceIdType.MESH,
        )
        if when is None:
            copy.start()
        else:
            pl.when(when)(lambda: copy.start())
        sent.append((copy, when))

    def arrived(dst, ssem, rsem, device):
        pltpu.make_async_remote_copy(
            src_ref=dst, dst_ref=dst, send_sem=ssem, recv_sem=rsem,
            device_id=device, device_id_type=pl.DeviceIdType.MESH,
        ).wait_recv()

    def fac_load(i, sem):
        return pltpu.make_async_copy(fac_hbm.at[i], fac.at[i], load_sem.at[sem])

    aff_loads = [
        pltpu.make_async_copy(aff_hbm.at[k], aff.at[k], load_sem.at[count + k])
        for k in range(tiles)
    ]
    order = [lax.rem(r + i, count) for i in range(count)]
    fac_loads = [fac_load(order[i], i) for i in range(count)]
    for copy in fac_loads:
        copy.start()
    for copy in aff_loads:
        copy.start()

    barrier = pltpu.get_barrier_semaphore()
    for side in (LEFT, RIGHT):
        @pl.when(has[side])
        def _():
            pl.semaphore_signal(
                barrier, inc=1, device_id=towards[side], device_id_type=pl.DeviceIdType.MESH
            )
    pl.semaphore_signal(barrier, inc=1, device_id=sibling, device_id_type=pl.DeviceIdType.MESH)
    for d in range(1, pairs):
        pl.semaphore_signal(
            barrier, inc=1, device_id=across(d), device_id_type=pl.DeviceIdType.MESH
        )

    def convert(i):
        fac_loads[i].wait()
        block = fac[order[i]].astype(jnp.bfloat16)
        held[order[i]] = block
        win[count + order[i]] = block

    convert(0)
    neighbours = jnp.where(has[LEFT], 1, 0) + jnp.where(has[RIGHT], 1, 0)
    pl.semaphore_wait(barrier, pairs + neighbours)

    for h, rows in enumerate(rows_of):
        for side in (LEFT, RIGHT):
            there = 1 - side
            send(
                held.at[r, rows], win.at[2 * count * there + r, rows],
                wx_s.at[side, h], wx_r.at[there, h], towards[side], has[side],
            )
    for side in (LEFT, RIGHT):
        @pl.when(jnp.logical_not(has[side]))
        def _():
            win[pl.ds(2 * count * side, count)] = jnp.zeros(
                (count, keypoints, universe), jnp.bfloat16
            )
            r3[side] = jnp.zeros((keypoints, universe), jnp.bfloat16)

    for i in range(1, count):
        convert(i)

    first = [pairs_ref[k, 0] - t * count for k in range(tiles)]
    second = [pairs_ref[k, 1] - (t - 1) * count for k in range(tiles)]
    for k in range(tiles):
        aff_loads[k].wait()
        back[k] = dot_t(aff[k], held[jnp.clip(first[k], 0, count - 1)])

    def partial(side, m, rows):
        slot = (0, 2 * count, count)[side] + m
        total = jnp.where(second[0] == slot, 1.0, 0.0) * back[0, rows]
        for k in range(1, tiles):
            total += jnp.where(second[k] == slot, 1.0, 0.0) * back[k, rows]
        if side == OWN:
            for k in range(tiles):
                total += jnp.where(first[k] == m, 1.0, 0.0) * forw[k, rows]
        return total

    def pair_send(side, h):
        rows = rows_of[h]
        for q in range(pairs):
            s1[side, h, q] = partial(side, 2 * q + (1 - c), rows).astype(jnp.bfloat16)
        send(
            s1.at[side, h], r1.at[side, h], g1_s.at[side, h], g1_r.at[side, h], sibling
        )

    def across_send(side, h):
        rows = rows_of[h]
        arrived(r1.at[side, h], g1_s.at[side, h], g1_r.at[side, h], sibling)
        for d in range(1, pairs):
            q = pair_at(d)
            s2[side, h, d - 1] = (
                partial(side, 2 * q + c, rows) + r1[side, h, q].astype(jnp.float32)
            ).astype(jnp.bfloat16)
            send(
                s2.at[side, h, d - 1], r2.at[side, h, d - 1],
                g2_s.at[side, h, d - 1], g2_r.at[side, h, d - 1], across(d),
            )

    def rep_sum(side, h):
        rows = rows_of[h]
        total = partial(side, r, rows) + r1[side, h, p].astype(jnp.float32)
        for d in range(1, pairs):
            arrived(
                r2.at[side, h, d - 1], g2_s.at[side, h, d - 1], g2_r.at[side, h, d - 1], across(d)
            )
            total += r2[side, h, d - 1].astype(jnp.float32)
        return total

    def window_slot(side, m, rows):
        return win.at[2 * count * side + m, rows]

    def window_out(h):
        rows = rows_of[h]
        for side in (LEFT, RIGHT):
            mine = window_slot(side, r, rows)

            @pl.when(has[side])
            def _():
                arrived(mine, wx_s.at[side, h], wx_r.at[side, h], towards[side])

            for d in range(1, pairs):
                send(
                    mine, mine, wy_s.at[side, h, d - 1], wy_r.at[side, h, d - 1],
                    across(d), has[side],
                )
            send(mine, mine, wc_s.at[side, h, 0], wc_r.at[side, h, 0], sibling, has[side])

    def window_pass(h):
        rows = rows_of[h]
        for side in (LEFT, RIGHT):
            for d in range(1, pairs):
                q = lax.rem(p - d + pairs, pairs)
                theirs = window_slot(side, 2 * q + c, rows)

                @pl.when(has[side])
                def _():
                    arrived(
                        theirs, wy_s.at[side, h, d - 1], wy_r.at[side, h, d - 1], across(d)
                    )

                send(
                    theirs, theirs, wc_s.at[side, h, d], wc_r.at[side, h, d], sibling, has[side]
                )

    def window_end(h):
        rows = rows_of[h]
        for side in (LEFT, RIGHT):
            for d in range(pairs):
                q = lax.rem(p - d + pairs, pairs)

                @pl.when(has[side])
                def _():
                    arrived(
                        window_slot(side, 2 * q + (1 - c), rows),
                        wc_s.at[side, h, d], wc_r.at[side, h, d], sibling,
                    )

    for h in range(CHUNKS):
        for side in (LEFT, RIGHT):
            pair_send(side, h)
    for h in range(CHUNKS):
        window_out(h)
        for side in (LEFT, RIGHT):
            across_send(side, h)
    for h in range(CHUNKS):
        window_pass(h)
        for side in (LEFT, RIGHT):
            s3[side, rows_of[h]] = rep_sum(side, h).astype(jnp.bfloat16)
            send(
                s3.at[side, rows_of[h]], r3.at[1 - side, rows_of[h]],
                g3_s.at[side, h], g3_r.at[1 - side, h], towards[side], has[side],
            )
    for h in range(CHUNKS):
        window_end(h)

    for h, rows in enumerate(rows_of):
        for k in range(tiles):
            forw[k, rows] = dot(aff[k, rows], win[jnp.clip(second[k], 0, 3 * count - 1)])
        pair_send(OWN, h)
    for h in range(CHUNKS):
        across_send(OWN, h)
    gram = None
    squares = None
    parts = []
    for h, rows in enumerate(rows_of):
        total = rep_sum(OWN, h)
        for side in (LEFT, RIGHT):
            @pl.when(has[side])
            def _():
                arrived(
                    r3.at[side, rows], g3_s.at[side, h], g3_r.at[side, h], towards[side]
                )
            total += r3[side, rows].astype(jnp.float32)
        ascended = fac[r, rows] + ascent_step * total
        asc[rows] = ascended
        high, low = split(ascended)
        cross = dot_t(high, low)
        part = dot_t(high, high) + (cross + cross.T)
        gram = part if gram is None else gram + part
        ss = jnp.sum(ascended * ascended)
        squares = ss if squares is None else squares + ss

    factor = start_scale * math.sqrt(universe) * lax.rsqrt(
        jnp.full((1, 1), squares, jnp.float32) + epsilon
    )
    gram = gram * (factor * factor)
    eye = (
        lax.broadcasted_iota(jnp.int32, (universe, universe), 0)
        == lax.broadcasted_iota(jnp.int32, (universe, universe), 1)
    ).astype(jnp.float32)
    product = None
    for step in range(NS_STEPS):
        mix = split(1.5 * eye - 0.5 * gram)
        if product is None:
            product = 1.5 * eye - 0.5 * gram
        else:
            product = dot3(split(product), mix)
        if step < NS_STEPS - 1:
            gram = dot3(split(dot3(split(gram), mix)), mix)
    product = split(product * (factor * math.sqrt(keypoints)))

    for h, rows in enumerate(rows_of):
        result = dot3(split(asc[rows]), product)
        own_ref[rows] = result
        out_ref[r, rows] = result.astype(jnp.bfloat16)
        mine = out_ref.at[r, rows]
        for d in range(1, pairs):
            send(mine, mine, oy_s.at[h, d - 1], oy_r.at[h, d - 1], across(d))
        send(mine, mine, oc_s.at[h, 0], oc_r.at[h, 0], sibling)
    for h, rows in enumerate(rows_of):
        for d in range(1, pairs):
            q = lax.rem(p - d + pairs, pairs)
            theirs = out_ref.at[2 * q + c, rows]
            arrived(theirs, oy_s.at[h, d - 1], oy_r.at[h, d - 1], across(d))
            send(theirs, theirs, oc_s.at[h, d], oc_r.at[h, d], sibling)
    for h, rows in enumerate(rows_of):
        for d in range(pairs):
            q = lax.rem(p - d + pairs, pairs)
            arrived(
                out_ref.at[2 * q + (1 - c), rows], oc_s.at[h, d], oc_r.at[h, d], sibling
            )
    for copy, when in sent:
        if when is None:
            copy.wait_send()
        else:
            pl.when(when)(lambda: copy.wait_send())


def shards(owners, rep, affinity, tile_pairs, factors):
    count, keypoints, universe = factors.shape
    tiles = affinity.shape[0]
    assert count == rep and rep % 2 == 0
    pairs = rep // 2
    half = keypoints // CHUNKS
    bf, f32 = jnp.bfloat16, jnp.float32
    image = (keypoints, universe)
    dma = pltpu.SemaphoreType.DMA
    C = CHUNKS
    D = max(pairs - 1, 1)
    gathered, own = pl.pallas_call(
        functools.partial(kernel, owners, rep),
        out_shape=(
            jax.ShapeDtypeStruct((count, *image), bf),
            jax.ShapeDtypeStruct(image, f32),
        ),
        in_specs=[
            pl.BlockSpec(memory_space=pltpu.SMEM),
            pl.BlockSpec(memory_space=pl.ANY),
            pl.BlockSpec(memory_space=pl.ANY),
        ],
        out_specs=(
            pl.BlockSpec(memory_space=pltpu.VMEM),
            pl.BlockSpec(memory_space=pltpu.VMEM),
        ),
        scratch_shapes=[
            pltpu.VMEM(affinity.shape, bf),
            pltpu.VMEM(factors.shape, f32),
            pltpu.VMEM(factors.shape, bf),
            pltpu.VMEM((3 * count, *image), bf),
            pltpu.VMEM((tiles, *image), f32),
            pltpu.VMEM((tiles, *image), f32),
            pltpu.VMEM((3, C, pairs, half, universe), bf),
            pltpu.VMEM((3, C, pairs, half, universe), bf),
            pltpu.VMEM((3, C, D, half, universe), bf),
            pltpu.VMEM((3, C, D, half, universe), bf),
            pltpu.VMEM((2, *image), bf),
            pltpu.VMEM((2, *image), bf),
            pltpu.VMEM(image, f32),
            dma((count + tiles,)),
            dma((2, C)), dma((2, C)),
            dma((2, C, D)), dma((2, C, D)),
            dma((2, C, pairs)), dma((2, C, pairs)),
            dma((3, C)), dma((3, C)),
            dma((3, C, D)), dma((3, C, D)),
            dma((2, C)), dma((2, C)),
            dma((C, D)), dma((C, D)),
            dma((C, pairs)), dma((C, pairs)),
        ],
        compiler_params=pltpu.CompilerParams(
            collective_id=0, has_side_effects=True, vmem_limit_bytes=48 * 1024 * 1024
        ),
    )(tile_pairs, affinity, factors)
    mine = lax.broadcasted_iota(jnp.int32, (count, 1, 1), 0) == lax.axis_index("rep")
    return jnp.where(mine, own[None], gathered.astype(f32))


def solution(mesh):
    in_specs = (P(("tiles", "rep"), None, None), P(("tiles", "rep"), None), P("tiles", None, None))
    out_specs = P("tiles", None, None)
    body = functools.partial(shards, mesh.shape["tiles"], mesh.shape["rep"])
    return jax.shard_map(body, mesh=mesh, in_specs=in_specs, out_specs=out_specs, check_vma=False)
```

```python
import functools
import math

import jax
import jax.numpy as jnp
from jax import lax
from jax.experimental import pallas as pl
from jax.experimental.pallas import tpu as pltpu
from jax.sharding import PartitionSpec as P

NS_STEPS = 6

epsilon = 1e-06
start_scale = 0.25
ascent_step = 0.25

CHUNKS = 2
LEFT, RIGHT, OWN = 0, 1, 2


def dot(a, b):
    return jnp.dot(a, b, preferred_element_type=jnp.float32)


def dot_t(a, b):
    return lax.dot_general(a, b, (((0,), (0,)), ((), ())), preferred_element_type=jnp.float32)


def split(x):
    high = x.astype(jnp.bfloat16)
    return high, (x - high.astype(jnp.float32)).astype(jnp.bfloat16)


def dot3(a, b):
    return dot(a[0], b[0]) + (dot(a[0], b[1]) + dot(a[1], b[0]))


def kernel(
    owners, rep, pairs_ref, aff_hbm, fac_hbm, out_ref, own_ref,
    aff, fac, held, win, back, forw, s1, r1, s2, r2, s3, r3, asc,
    load_sem, wx_s, wx_r, wy_s, wy_r, wc_s, wc_r,
    g1_s, g1_r, g2_s, g2_r, g3_s, g3_r, oy_s, oy_r, oc_s, oc_r,
):
    count, keypoints, universe = fac.shape
    tiles = aff.shape[0]
    pairs = rep // 2
    t = lax.axis_index("tiles")
    r = lax.axis_index("rep")
    p, c = r // 2, r % 2
    sibling = {"rep": 2 * p + (1 - c)}
    has = (t > 0, t < owners - 1)
    towards = ({"tiles": t - 1}, {"tiles": t + 1})
    odd = lax.rem(t, 2)
    near, onward = t + 1 - 2 * odd, 2 - 4 * odd
    near_base, far_base = 2 * count * (1 - odd), 2 * count * odd
    passes = (t + onward >= 0) & (t + onward < owners)
    fed = (t - onward >= 0) & (t - onward < owners)
    rows_of = [
        pl.ds(i * (keypoints // CHUNKS), keypoints // CHUNKS) for i in range(CHUNKS)
    ]
    sent = []

    def pair_at(d):
        return lax.rem(p + d, pairs)

    def across(d):
        return {"rep": 2 * pair_at(d) + c}

    def send(src, dst, ssem, rsem, device, when=None):
        copy = pltpu.make_async_remote_copy(
            src_ref=src, dst_ref=dst, send_sem=ssem, recv_sem=rsem,
            device_id=device, device_id_type=pl.DeviceIdType.MESH,
        )
        if when is None:
            copy.start()
        else:
            pl.when(when)(lambda: copy.start())
        sent.append((copy, when))

    def arrived(dst, ssem, rsem, device):
        pltpu.make_async_remote_copy(
            src_ref=dst, dst_ref=dst, send_sem=ssem, recv_sem=rsem,
            device_id=device, device_id_type=pl.DeviceIdType.MESH,
        ).wait_recv()

    def fac_load(i, sem):
        return pltpu.make_async_copy(fac_hbm.at[i], fac.at[i], load_sem.at[sem])

    aff_loads = [
        pltpu.make_async_copy(aff_hbm.at[k], aff.at[k], load_sem.at[count + k])
        for k in range(tiles)
    ]
    order = [2 * q + c for q in range(pairs)] + [2 * q + (1 - c) for q in range(pairs)]
    fac_loads = [fac_load(order[i], i) for i in range(count)]
    for copy in fac_loads:
        copy.start()
    for copy in aff_loads:
        copy.start()

    barrier = pltpu.get_barrier_semaphore()
    beside = pairs
    for other in (t - 1, t + 1, t - 2, t + 2):
        there = (other >= 0) & (other < owners)
        beside += jnp.where(there, 1, 0)

        @pl.when(there)
        def _():
            pl.semaphore_signal(
                barrier, inc=1, device_id={"tiles": other}, device_id_type=pl.DeviceIdType.MESH
            )
    pl.semaphore_signal(barrier, inc=1, device_id=sibling, device_id_type=pl.DeviceIdType.MESH)
    for d in range(1, pairs):
        pl.semaphore_signal(
            barrier, inc=1, device_id=across(d), device_id_type=pl.DeviceIdType.MESH
        )

    def convert(i):
        fac_loads[i].wait()
        block = fac[order[i]].astype(jnp.bfloat16)
        held[order[i]] = block
        win[count + order[i]] = block

    for i in range(pairs):
        convert(i)
    pl.semaphore_wait(barrier, beside)

    pieces = [(q, h) for q in range(pairs) for h in range(CHUNKS)]
    for q, h in pieces:
        send(
            held.at[2 * q + c, rows_of[h]], win.at[far_base + 2 * q + c, rows_of[h]],
            wx_s.at[q, h], wx_r.at[q, h], {"tiles": near},
        )
    for side in (LEFT, RIGHT):
        @pl.when(jnp.logical_not(has[side]))
        def _():
            win[pl.ds(2 * count * side, count)] = jnp.zeros(
                (count, keypoints, universe), jnp.bfloat16
            )
            r3[side] = jnp.zeros((keypoints, universe), jnp.bfloat16)

    for i in range(pairs, count):
        convert(i)

    first = [pairs_ref[k, 0] - t * count for k in range(tiles)]
    second = [pairs_ref[k, 1] - (t - 1) * count for k in range(tiles)]
    for k in range(tiles):
        aff_loads[k].wait()
        back[k] = dot_t(aff[k], held[jnp.clip(first[k], 0, count - 1)])

    def partial(side, m, rows):
        slot = (0, 2 * count, count)[side] + m
        total = jnp.where(second[0] == slot, 1.0, 0.0) * back[0, rows]
        for k in range(1, tiles):
            total += jnp.where(second[k] == slot, 1.0, 0.0) * back[k, rows]
        if side == OWN:
            for k in range(tiles):
                total += jnp.where(first[k] == m, 1.0, 0.0) * forw[k, rows]
        return total

    def pair_send(side, h):
        rows = rows_of[h]
        for q in range(pairs):
            s1[side, h, q] = partial(side, 2 * q + (1 - c), rows).astype(jnp.bfloat16)
        send(
            s1.at[side, h], r1.at[side, h], g1_s.at[side, h], g1_r.at[side, h], sibling
        )

    def across_send(side, h):
        rows = rows_of[h]
        arrived(r1.at[side, h], g1_s.at[side, h], g1_r.at[side, h], sibling)
        for d in range(1, pairs):
            q = pair_at(d)
            s2[side, h, d - 1] = (
                partial(side, 2 * q + c, rows) + r1[side, h, q].astype(jnp.float32)
            ).astype(jnp.bfloat16)
            send(
                s2.at[side, h, d - 1], r2.at[side, h, d - 1],
                g2_s.at[side, h, d - 1], g2_r.at[side, h, d - 1], across(d),
            )

    def rep_sum(side, h):
        rows = rows_of[h]
        total = partial(side, r, rows) + r1[side, h, p].astype(jnp.float32)
        for d in range(1, pairs):
            arrived(
                r2.at[side, h, d - 1], g2_s.at[side, h, d - 1], g2_r.at[side, h, d - 1], across(d)
            )
            total += r2[side, h, d - 1].astype(jnp.float32)
        return total

    def window_near(q, h):
        m, rows = 2 * q + c, rows_of[h]
        slot = win.at[near_base + m, rows]
        arrived(slot, wx_s.at[q, h], wx_r.at[q, h], {"tiles": near})
        send(
            slot, win.at[far_base + m, rows], wy_s.at[q, h], wy_r.at[q, h],
            {"tiles": t + onward}, passes,
        )
        send(slot, slot, wc_s.at[0, q, h], wc_r.at[0, q, h], sibling)

    def window_far(q, h):
        slot = win.at[far_base + 2 * q + c, rows_of[h]]

        @pl.when(fed)
        def _():
            arrived(slot, wy_s.at[q, h], wy_r.at[q, h], {"tiles": t - onward})

        send(slot, slot, wc_s.at[1, q, h], wc_r.at[1, q, h], sibling, fed)

    def window_end(q, h):
        m, rows = 2 * q + (1 - c), rows_of[h]
        arrived(win.at[near_base + m, rows], wc_s.at[0, q, h], wc_r.at[0, q, h], sibling)

        @pl.when(fed)
        def _():
            arrived(win.at[far_base + m, rows], wc_s.at[1, q, h], wc_r.at[1, q, h], sibling)

    for h in range(CHUNKS):
        for side in (LEFT, RIGHT):
            pair_send(side, h)
    split_at = len(pieces) // 2
    for h in range(CHUNKS):
        for side in (LEFT, RIGHT):
            across_send(side, h)
        if h < split_at:
            window_near(*pieces[h])
    for piece in pieces[min(CHUNKS, split_at):]:
        window_near(*piece)
    for h in range(CHUNKS):
        for side in (LEFT, RIGHT):
            s3[side, rows_of[h]] = rep_sum(side, h).astype(jnp.bfloat16)
            send(
                s3.at[side, rows_of[h]], r3.at[1 - side, rows_of[h]],
                g3_s.at[side, h], g3_r.at[1 - side, h], towards[side], has[side],
            )
        window_far(*pieces[h])
    for piece in pieces[CHUNKS:]:
        window_far(*piece)
    for piece in pieces:
        window_end(*piece)

    for h, rows in enumerate(rows_of):
        for k in range(tiles):
            forw[k, rows] = dot(aff[k, rows], win[jnp.clip(second[k], 0, 3 * count - 1)])
        pair_send(OWN, h)
    for h in range(CHUNKS):
        across_send(OWN, h)
    gram = None
    squares = None
    parts = []
    for h, rows in enumerate(rows_of):
        total = rep_sum(OWN, h)
        for side in (LEFT, RIGHT):
            @pl.when(has[side])
            def _():
                arrived(
                    r3.at[side, rows], g3_s.at[side, h], g3_r.at[side, h], towards[side]
                )
            total += r3[side, rows].astype(jnp.float32)
        ascended = fac[r, rows] + ascent_step * total
        asc[rows] = ascended
        high, low = split(ascended)
        cross = dot_t(high, low)
        part = dot_t(high, high) + (cross + cross.T)
        gram = part if gram is None else gram + part
        ss = jnp.sum(ascended * ascended)
        squares = ss if squares is None else squares + ss

    factor = start_scale * math.sqrt(universe) * lax.rsqrt(
        jnp.full((1, 1), squares, jnp.float32) + epsilon
    )
    gram = gram * (factor * factor)
    eye = (
        lax.broadcasted_iota(jnp.int32, (universe, universe), 0)
        == lax.broadcasted_iota(jnp.int32, (universe, universe), 1)
    ).astype(jnp.float32)
    product = None
    for step in range(NS_STEPS):
        mix = split(1.5 * eye - 0.5 * gram)
        if product is None:
            product = 1.5 * eye - 0.5 * gram
        else:
            product = dot3(split(product), mix)
        if step < NS_STEPS - 1:
            gram = dot3(split(dot3(split(gram), mix)), mix)
    product = split(product * (factor * math.sqrt(keypoints)))

    for h, rows in enumerate(rows_of):
        result = dot3(split(asc[rows]), product)
        own_ref[rows] = result
        out_ref[r, rows] = result.astype(jnp.bfloat16)
        mine = out_ref.at[r, rows]
        for d in range(1, pairs):
            send(mine, mine, oy_s.at[h, d - 1], oy_r.at[h, d - 1], across(d))
        send(mine, mine, oc_s.at[h, 0], oc_r.at[h, 0], sibling)
    for h, rows in enumerate(rows_of):
        for d in range(1, pairs):
            q = lax.rem(p - d + pairs, pairs)
            theirs = out_ref.at[2 * q + c, rows]
            arrived(theirs, oy_s.at[h, d - 1], oy_r.at[h, d - 1], across(d))
            send(theirs, theirs, oc_s.at[h, d], oc_r.at[h, d], sibling)
    for h, rows in enumerate(rows_of):
        for d in range(pairs):
            q = lax.rem(p - d + pairs, pairs)
            arrived(
                out_ref.at[2 * q + (1 - c), rows], oc_s.at[h, d], oc_r.at[h, d], sibling
            )
    for copy, when in sent:
        if when is None:
            copy.wait_send()
        else:
            pl.when(when)(lambda: copy.wait_send())


def shards(owners, rep, affinity, tile_pairs, factors):
    count, keypoints, universe = factors.shape
    tiles = affinity.shape[0]
    assert count == rep and rep % 2 == 0
    pairs = rep // 2
    half = keypoints // CHUNKS
    bf, f32 = jnp.bfloat16, jnp.float32
    image = (keypoints, universe)
    dma = pltpu.SemaphoreType.DMA
    C = CHUNKS
    D = max(pairs - 1, 1)
    gathered, own = pl.pallas_call(
        functools.partial(kernel, owners, rep),
        out_shape=(
            jax.ShapeDtypeStruct((count, *image), bf),
            jax.ShapeDtypeStruct(image, f32),
        ),
        in_specs=[
            pl.BlockSpec(memory_space=pltpu.SMEM),
            pl.BlockSpec(memory_space=pltpu.HBM),
            pl.BlockSpec(memory_space=pltpu.HBM),
        ],
        out_specs=(
            pl.BlockSpec(memory_space=pltpu.VMEM),
            pl.BlockSpec(memory_space=pltpu.VMEM),
        ),
        scratch_shapes=[
            pltpu.VMEM(affinity.shape, bf),
            pltpu.VMEM(factors.shape, f32),
            pltpu.VMEM(factors.shape, bf),
            pltpu.VMEM((3 * count, *image), bf),
            pltpu.VMEM((tiles, *image), f32),
            pltpu.VMEM((tiles, *image), f32),
            pltpu.VMEM((3, C, pairs, half, universe), bf),
            pltpu.VMEM((3, C, pairs, half, universe), bf),
            pltpu.VMEM((3, C, D, half, universe), bf),
            pltpu.VMEM((3, C, D, half, universe), bf),
            pltpu.VMEM((2, *image), bf),
            pltpu.VMEM((2, *image), bf),
            pltpu.VMEM(image, f32),
            dma((count + tiles,)),
            dma((pairs, C)), dma((pairs, C)),
            dma((pairs, C)), dma((pairs, C)),
            dma((2, pairs, C)), dma((2, pairs, C)),
            dma((3, C)), dma((3, C)),
            dma((3, C, D)), dma((3, C, D)),
            dma((2, C)), dma((2, C)),
            dma((C, D)), dma((C, D)),
            dma((C, pairs)), dma((C, pairs)),
        ],
        compiler_params=pltpu.CompilerParams(
            collective_id=0, has_side_effects=True, vmem_limit_bytes=48 * 1024 * 1024
        ),
    )(tile_pairs, affinity, factors)
    mine = lax.broadcasted_iota(jnp.int32, (count, 1, 1), 0) == lax.axis_index("rep")
    return jnp.where(mine, own[None], gathered.astype(f32))


def solution(mesh):
    in_specs = (P(("tiles", "rep"), None, None), P(("tiles", "rep"), None), P("tiles", None, None))
    out_specs = P("tiles", None, None)
    body = functools.partial(shards, mesh.shape["tiles"], mesh.shape["rep"])
    return jax.shard_map(body, mesh=mesh, in_specs=in_specs, out_specs=out_specs, check_vma=False)
```

```python
import functools
import math

import jax
import jax.numpy as jnp
from jax import lax
from jax.experimental import pallas as pl
from jax.experimental.pallas import tpu as pltpu
from jax.sharding import PartitionSpec as P

NS_STEPS = 6

epsilon = 1e-06
start_scale = 0.25
ascent_step = 0.25

CHUNKS = 2
LEFT, RIGHT, OWN = 0, 1, 2


def dot(a, b):
    return jnp.dot(a, b, preferred_element_type=jnp.float32)


def dot_t(a, b):
    return lax.dot_general(a, b, (((0,), (0,)), ((), ())), preferred_element_type=jnp.float32)


def split(x):
    high = x.astype(jnp.bfloat16)
    return high, (x - high.astype(jnp.float32)).astype(jnp.bfloat16)


def dot3(a, b):
    return dot(a[0], b[0]) + (dot(a[0], b[1]) + dot(a[1], b[0]))


def kernel(
    owners, rep, pairs_ref, aff_hbm, fac_hbm, out_ref, own_ref,
    aff, fac, held, win, back, forw, s1, r1, s2, r2, s3, r3, asc,
    load_sem, wx_s, wx_r, wy_s, wy_r, wc_s, wc_r,
    g1_s, g1_r, g2_s, g2_r, g3_s, g3_r, oy_s, oy_r, oc_s, oc_r,
):
    count, keypoints, universe = fac.shape
    tiles = aff.shape[0]
    pairs = rep // 2
    t = lax.axis_index("tiles")
    r = lax.axis_index("rep")
    p, c = r // 2, r % 2
    sibling = {"rep": 2 * p + (1 - c)}
    has = (t > 0, t < owners - 1)
    towards = ({"tiles": t - 1}, {"tiles": t + 1})
    odd = lax.rem(t, 2)
    near, onward = t + 1 - 2 * odd, 2 - 4 * odd
    near_base, far_base = 2 * count * (1 - odd), 2 * count * odd
    passes = (t + onward >= 0) & (t + onward < owners)
    fed = (t - onward >= 0) & (t - onward < owners)
    rows_of = [
        pl.ds(i * (keypoints // CHUNKS), keypoints // CHUNKS) for i in range(CHUNKS)
    ]
    sent = []

    def pair_at(d):
        return lax.rem(p + d, pairs)

    def across(d):
        return {"rep": 2 * pair_at(d) + c}

    def send(src, dst, ssem, rsem, device, when=None):
        copy = pltpu.make_async_remote_copy(
            src_ref=src, dst_ref=dst, send_sem=ssem, recv_sem=rsem,
            device_id=device, device_id_type=pl.DeviceIdType.MESH,
        )
        if when is None:
            copy.start()
        else:
            pl.when(when)(lambda: copy.start())
        sent.append((copy, when))

    def arrived(dst, ssem, rsem, device):
        pltpu.make_async_remote_copy(
            src_ref=dst, dst_ref=dst, send_sem=ssem, recv_sem=rsem,
            device_id=device, device_id_type=pl.DeviceIdType.MESH,
        ).wait_recv()

    def fac_load(i, sem):
        return pltpu.make_async_copy(fac_hbm.at[i], fac.at[i], load_sem.at[sem])

    aff_loads = [
        pltpu.make_async_copy(aff_hbm.at[k], aff.at[k], load_sem.at[count + k])
        for k in range(tiles)
    ]
    order = [2 * q + c for q in range(pairs)] + [2 * q + (1 - c) for q in range(pairs)]
    fac_loads = [fac_load(order[i], i) for i in range(count)]
    for copy in fac_loads:
        copy.start()
    for copy in aff_loads:
        copy.start()

    barrier = pltpu.get_barrier_semaphore()
    beside = pairs
    for other in (t - 1, t + 1, t - 2, t + 2):
        there = (other >= 0) & (other < owners)
        beside += jnp.where(there, 1, 0)

        @pl.when(there)
        def _():
            pl.semaphore_signal(
                barrier, inc=1, device_id={"tiles": other}, device_id_type=pl.DeviceIdType.MESH
            )
    pl.semaphore_signal(barrier, inc=1, device_id=sibling, device_id_type=pl.DeviceIdType.MESH)
    for d in range(1, pairs):
        pl.semaphore_signal(
            barrier, inc=1, device_id=across(d), device_id_type=pl.DeviceIdType.MESH
        )

    def convert(i):
        fac_loads[i].wait()
        block = fac[order[i]].astype(jnp.bfloat16)
        held[order[i]] = block
        win[count + order[i]] = block

    for i in range(pairs):
        convert(i)
    pl.semaphore_wait(barrier, beside)

    pieces = [(q, h) for q in range(pairs) for h in range(CHUNKS)]
    for q, h in pieces:
        send(
            held.at[2 * q + c, rows_of[h]], win.at[far_base + 2 * q + c, rows_of[h]],
            wx_s.at[q, h], wx_r.at[q, h], {"tiles": near},
        )
    for side in (LEFT, RIGHT):
        @pl.when(jnp.logical_not(has[side]))
        def _():
            win[pl.ds(2 * count * side, count)] = jnp.zeros(
                (count, keypoints, universe), jnp.bfloat16
            )
            r3[side] = jnp.zeros((keypoints, universe), jnp.bfloat16)

    for i in range(pairs, count):
        convert(i)

    first = [pairs_ref[k, 0] - t * count for k in range(tiles)]
    second = [pairs_ref[k, 1] - (t - 1) * count for k in range(tiles)]
    for k in range(tiles):
        aff_loads[k].wait()

    def backward(h):
        for k in range(tiles):
            back[k, rows_of[h]] = dot_t(
                aff[k, :, rows_of[h]], held[jnp.clip(first[k], 0, count - 1)]
            )

    def partial(side, m, rows):
        slot = (0, 2 * count, count)[side] + m
        total = jnp.where(second[0] == slot, 1.0, 0.0) * back[0, rows]
        for k in range(1, tiles):
            total += jnp.where(second[k] == slot, 1.0, 0.0) * back[k, rows]
        if side == OWN:
            for k in range(tiles):
                total += jnp.where(first[k] == m, 1.0, 0.0) * forw[k, rows]
        return total

    def pair_send(side, h):
        rows = rows_of[h]
        for q in range(pairs):
            s1[side, h, q] = partial(side, 2 * q + (1 - c), rows).astype(jnp.bfloat16)
        send(
            s1.at[side, h], r1.at[side, h], g1_s.at[side, h], g1_r.at[side, h], sibling
        )

    def across_send(side, h):
        rows = rows_of[h]
        arrived(r1.at[side, h], g1_s.at[side, h], g1_r.at[side, h], sibling)
        for d in range(1, pairs):
            q = pair_at(d)
            s2[side, h, d - 1] = (
                partial(side, 2 * q + c, rows) + r1[side, h, q].astype(jnp.float32)
            ).astype(jnp.bfloat16)
            send(
                s2.at[side, h, d - 1], r2.at[side, h, d - 1],
                g2_s.at[side, h, d - 1], g2_r.at[side, h, d - 1], across(d),
            )

    def rep_sum(side, h):
        rows = rows_of[h]
        total = partial(side, r, rows) + r1[side, h, p].astype(jnp.float32)
        for d in range(1, pairs):
            arrived(
                r2.at[side, h, d - 1], g2_s.at[side, h, d - 1], g2_r.at[side, h, d - 1], across(d)
            )
            total += r2[side, h, d - 1].astype(jnp.float32)
        return total

    def window_near(q, h):
        m, rows = 2 * q + c, rows_of[h]
        slot = win.at[near_base + m, rows]
        arrived(slot, wx_s.at[q, h], wx_r.at[q, h], {"tiles": near})
        send(
            slot, win.at[far_base + m, rows], wy_s.at[q, h], wy_r.at[q, h],
            {"tiles": t + onward}, passes,
        )
        send(slot, slot, wc_s.at[0, q, h], wc_r.at[0, q, h], sibling)

    def window_far(q, h):
        slot = win.at[far_base + 2 * q + c, rows_of[h]]

        @pl.when(fed)
        def _():
            arrived(slot, wy_s.at[q, h], wy_r.at[q, h], {"tiles": t - onward})

        send(slot, slot, wc_s.at[1, q, h], wc_r.at[1, q, h], sibling, fed)

    def window_end(q, h):
        m, rows = 2 * q + (1 - c), rows_of[h]
        arrived(win.at[near_base + m, rows], wc_s.at[0, q, h], wc_r.at[0, q, h], sibling)

        @pl.when(fed)
        def _():
            arrived(win.at[far_base + m, rows], wc_s.at[1, q, h], wc_r.at[1, q, h], sibling)

    split_at = len(pieces) // 2
    backward(0)
    for h in range(CHUNKS):
        for side in (LEFT, RIGHT):
            pair_send(side, h)
        if h + 1 < CHUNKS:
            backward(h + 1)
        for side in (LEFT, RIGHT):
            across_send(side, h)
        if h < split_at:
            window_near(*pieces[h])
    for piece in pieces[min(CHUNKS, split_at):]:
        window_near(*piece)
    for h in range(CHUNKS):
        for side in (LEFT, RIGHT):
            s3[side, rows_of[h]] = rep_sum(side, h).astype(jnp.bfloat16)
            send(
                s3.at[side, rows_of[h]], r3.at[1 - side, rows_of[h]],
                g3_s.at[side, h], g3_r.at[1 - side, h], towards[side], has[side],
            )
        window_far(*pieces[h])
    for piece in pieces[CHUNKS:]:
        window_far(*piece)
    for piece in pieces:
        window_end(*piece)

    for h, rows in enumerate(rows_of):
        for k in range(tiles):
            forw[k, rows] = dot(aff[k, rows], win[jnp.clip(second[k], 0, 3 * count - 1)])
        pair_send(OWN, h)
    for h in range(CHUNKS):
        across_send(OWN, h)
    gram = None
    squares = None
    parts = []
    for h, rows in enumerate(rows_of):
        total = rep_sum(OWN, h)
        for side in (LEFT, RIGHT):
            @pl.when(has[side])
            def _():
                arrived(
                    r3.at[side, rows], g3_s.at[side, h], g3_r.at[side, h], towards[side]
                )
            total += r3[side, rows].astype(jnp.float32)
        ascended = fac[r, rows] + ascent_step * total
        asc[rows] = ascended
        high, low = split(ascended)
        cross = dot_t(high, low)
        part = dot_t(high, high) + (cross + cross.T)
        gram = part if gram is None else gram + part
        ss = jnp.sum(ascended * ascended)
        squares = ss if squares is None else squares + ss

    factor = start_scale * math.sqrt(universe) * lax.rsqrt(
        jnp.full((1, 1), squares, jnp.float32) + epsilon
    )
    gram = gram * (factor * factor)
    eye = (
        lax.broadcasted_iota(jnp.int32, (universe, universe), 0)
        == lax.broadcasted_iota(jnp.int32, (universe, universe), 1)
    ).astype(jnp.float32)
    product = None
    for step in range(NS_STEPS):
        mix = split(1.5 * eye - 0.5 * gram)
        if product is None:
            product = 1.5 * eye - 0.5 * gram
        else:
            product = dot3(split(product), mix)
        if step < NS_STEPS - 1:
            gram = dot3(split(dot3(split(gram), mix)), mix)
    product = split(product * (factor * math.sqrt(keypoints)))

    for h, rows in enumerate(rows_of):
        result = dot3(split(asc[rows]), product)
        own_ref[rows] = result
        out_ref[r, rows] = result.astype(jnp.bfloat16)
        mine = out_ref.at[r, rows]
        for d in range(1, pairs):
            send(mine, mine, oy_s.at[h, d - 1], oy_r.at[h, d - 1], across(d))
        send(mine, mine, oc_s.at[h, 0], oc_r.at[h, 0], sibling)
    for h, rows in enumerate(rows_of):
        for d in range(1, pairs):
            q = lax.rem(p - d + pairs, pairs)
            theirs = out_ref.at[2 * q + c, rows]
            arrived(theirs, oy_s.at[h, d - 1], oy_r.at[h, d - 1], across(d))
            send(theirs, theirs, oc_s.at[h, d], oc_r.at[h, d], sibling)
    for h, rows in enumerate(rows_of):
        for d in range(pairs):
            q = lax.rem(p - d + pairs, pairs)
            arrived(
                out_ref.at[2 * q + (1 - c), rows], oc_s.at[h, d], oc_r.at[h, d], sibling
            )
    for copy, when in sent:
        if when is None:
            copy.wait_send()
        else:
            pl.when(when)(lambda: copy.wait_send())


def shards(owners, rep, affinity, tile_pairs, factors):
    count, keypoints, universe = factors.shape
    tiles = affinity.shape[0]
    assert count == rep and rep % 2 == 0
    pairs = rep // 2
    half = keypoints // CHUNKS
    bf, f32 = jnp.bfloat16, jnp.float32
    image = (keypoints, universe)
    dma = pltpu.SemaphoreType.DMA
    C = CHUNKS
    D = max(pairs - 1, 1)
    gathered, own = pl.pallas_call(
        functools.partial(kernel, owners, rep),
        out_shape=(
            jax.ShapeDtypeStruct((count, *image), bf),
            jax.ShapeDtypeStruct(image, f32),
        ),
        in_specs=[
            pl.BlockSpec(memory_space=pltpu.SMEM),
            pl.BlockSpec(memory_space=pltpu.HBM),
            pl.BlockSpec(memory_space=pltpu.HBM),
        ],
        out_specs=(
            pl.BlockSpec(memory_space=pltpu.VMEM),
            pl.BlockSpec(memory_space=pltpu.VMEM),
        ),
        scratch_shapes=[
            pltpu.VMEM(affinity.shape, bf),
            pltpu.VMEM(factors.shape, f32),
            pltpu.VMEM(factors.shape, bf),
            pltpu.VMEM((3 * count, *image), bf),
            pltpu.VMEM((tiles, *image), f32),
            pltpu.VMEM((tiles, *image), f32),
            pltpu.VMEM((3, C, pairs, half, universe), bf),
            pltpu.VMEM((3, C, pairs, half, universe), bf),
            pltpu.VMEM((3, C, D, half, universe), bf),
            pltpu.VMEM((3, C, D, half, universe), bf),
            pltpu.VMEM((2, *image), bf),
            pltpu.VMEM((2, *image), bf),
            pltpu.VMEM(image, f32),
            dma((count + tiles,)),
            dma((pairs, C)), dma((pairs, C)),
            dma((pairs, C)), dma((pairs, C)),
            dma((2, pairs, C)), dma((2, pairs, C)),
            dma((3, C)), dma((3, C)),
            dma((3, C, D)), dma((3, C, D)),
            dma((2, C)), dma((2, C)),
            dma((C, D)), dma((C, D)),
            dma((C, pairs)), dma((C, pairs)),
        ],
        compiler_params=pltpu.CompilerParams(
            collective_id=0, has_side_effects=True, vmem_limit_bytes=48 * 1024 * 1024
        ),
    )(tile_pairs, affinity, factors)
    mine = lax.broadcasted_iota(jnp.int32, (count, 1, 1), 0) == lax.axis_index("rep")
    return jnp.where(mine, own[None], gathered.astype(f32))


def solution(mesh):
    in_specs = (P(("tiles", "rep"), None, None), P(("tiles", "rep"), None), P("tiles", None, None))
    out_specs = P("tiles", None, None)
    body = functools.partial(shards, mesh.shape["tiles"], mesh.shape["rep"])
    return jax.shard_map(body, mesh=mesh, in_specs=in_specs, out_specs=out_specs, check_vma=False)
```
